128 devices in a mesh: elec: 8 (over y, x_hi), slab: 16 (over x_lo, z, core).
Axes of the slice: x: 4 (x_hi: 2, x_lo: 2; x = x_hi * 2 + x_lo), y: 4, z: 4, core: 2. Of those that a mesh axis runs over, the one named last changes fastest.
Arguments:
- secondary: bfloat16 [256, 64, 64, 128], P('elec', None, 'slab'), may hold values from -3 to 3
- conductivity: float32 [64, 64, 128], P('elec', 'slab'), may hold values from 0.1 to 10
- positions: int32 [3, 256], P(None, 'elec'), may hold values from 0 to 127, as said below
- pairs: int32 [32768, 2], replicated, may hold values from 0 to 255
- weights: float32 [32768], replicated, may hold values from -0.015625 to 0.015625
Outputs:
- sensitivity: float32 [64, 64, 128], P('elec', 'slab')
The draws below stay inside these ranges and needn't reach their ends.
Inputs may be any that keep to these rules, and one draw needn't show every extreme that they name: `positions`: row 0 is below 64, row 1 below 64, row 2 below 128.
All inputs are finite; a program needn't handle non-finite values.
Results may differ from the reference program's by a relative error of at most 0.018.
Values may be sent and summed in bfloat16 or wider, within the bound.
No kernel may reach another device: no remote copies, remote signals or barrier semaphores. Data moves between devices by JAX's collectives and lax.ppermute only.
A program may use at most 320 MiB of HBM per device.

```python
import math
import jax
import jax.numpy as jnp
from jax import lax

NX = 64
NY = 128
E = 256
PAIRS = 32768
NZ = 64


def draw_positions(key, part):
    key = jax.random.fold_in(key, 7)
    first_key, second_key, third_key = jax.random.split(key, 3)
    x_nodes = jax.random.randint(first_key, (E,), 0, NX)
    z_nodes = jax.random.randint(second_key, (E,), 0, NZ)
    y_nodes = jax.random.randint(third_key, (E,), 0, NY)
    return jnp.stack([x_nodes, z_nodes, y_nodes]).astype(jnp.int32)


def touch_ends(array, own_key, low, high):
    extent = array.shape
    place = [jax.random.randint(jax.random.fold_in(own_key, axis), (), 0, extent[axis]) for axis in range(len(extent))]
    array = array.at[tuple(place)].set(low)
    longest = extent.index(max(extent))
    place[longest] = (place[longest] + 1) % extent[longest]
    return array.at[tuple(place)].set(high)


def steps_of(key, extent, shards, low, largest):
    loudness, own = 1.0, jax.random.fold_in(key, 6)
    for axis_at, blocks in shards:
        heights = jnp.exp(jax.random.uniform(jax.random.fold_in(own, axis_at), (blocks,), jnp.float32, low / len(shards), largest / len(shards)))
        loudness = loudness * jnp.repeat(heights, extent[axis_at] // blocks).reshape([-1 if axis == axis_at else 1 for axis in range(len(extent))])
    return loudness


def scatter_about(key, extent, width, reach, shards=(), kind=jnp.bfloat16):
    array = jax.random.normal(key, extent, jnp.float32) * width
    if len(shards) > 0:
        array = steps_of(key, extent, shards, -0.22, 0.18) * array
    return jnp.clip(array, min=-reach, max=reach).astype(kind)


def setup_inputs(seed: int = 0) -> dict:
    streams_of = jax.random.split(jax.random.key(seed), 6)
    secondary = scatter_about(streams_of[0], (E, NX, NZ, NY), 0.5, 3.0, ((0, 8), (2, 16)))
    conductivity = jnp.clip(jnp.exp(math.log(10.0) - 4.6051702 * jax.random.uniform(streams_of[1], (NX, NZ, NY), jnp.float32) ** steps_of(streams_of[1], (NX, NZ, NY), ((0, 8), (1, 16)), -0.2, 0.2)), 0.1, 10.0)
    positions = draw_positions(jax.random.fold_in(streams_of[5], 71), 0)
    pairs = touch_ends(jax.random.randint(streams_of[3], (PAIRS, 2), 0, E), jax.random.fold_in(streams_of[3], 1), 0, E - 1).astype(jnp.int32)
    weights = scatter_about(streams_of[4], (PAIRS,), (1.0 / E), 0.015625, (), jnp.float32)
    return dict(secondary=secondary, conductivity=conductivity, positions=positions, pairs=pairs, weights=weights)


def pair_matrix(pairs, weights, count):
    flat = pairs[:, 0] * count + pairs[:, 1]
    summed = jax.ops.segment_sum(weights.astype(jnp.float32), flat, num_segments=count * count)
    return summed.reshape(count, count).astype(jnp.bfloat16)

def potential(secondary, positions, x_first, z_first):
    places = positions.astype(jnp.float32)
    x_coord = (jnp.arange(secondary.shape[1], dtype=jnp.int32) + x_first).astype(jnp.float32)
    z_coord = (jnp.arange(secondary.shape[2], dtype=jnp.int32) + z_first).astype(jnp.float32)
    y_coord = jnp.arange(secondary.shape[3], dtype=jnp.int32).astype(jnp.float32)
    x_gap = x_coord[None, :] - places[0][:, None]
    z_gap = z_coord[None, :] - places[1][:, None]
    y_gap = y_coord[None, :] - places[2][:, None]
    dist_sq = (x_gap * x_gap)[:, :, None, None] + (z_gap * z_gap)[:, None, :, None] + (y_gap * y_gap)[:, None, None, :]
    return (secondary.astype(jnp.float32) + 4.0 * lax.rsqrt(dist_sq + 0.5)).astype(jnp.bfloat16)

def slopes(block):
    center = block[:, :-1, :-1]
    slope_x = block[:, 1:, :-1] - center
    slope_z = block[:, :-1, 1:] - center
    slope_y = jnp.concatenate([center[..., 1:], jnp.zeros_like(center[..., :1])], axis=-1) - center
    return (slope_x.astype(jnp.bfloat16), slope_z.astype(jnp.bfloat16), slope_y.astype(jnp.bfloat16))

def reference(secondary, conductivity, positions, pairs, weights):
    fields = potential(secondary, positions, 0, 0)
    padded = jnp.pad(fields, ((0, 0), (0, 1), (0, 1), (0, 0)))
    pair_weights = pair_matrix(pairs, weights, E).astype(jnp.float32)
    count = fields.shape[0]

    def one_plane(x_index):
        block = lax.dynamic_slice_in_dim(padded, x_index, 2, 1).astype(jnp.float32)
        total = jnp.zeros(fields.shape[2:], jnp.float32)
        for slope in slopes(block):
            flat = slope.astype(jnp.float32).reshape(count, -1)
            mixed = jnp.dot(pair_weights, flat, precision=lax.Precision.HIGHEST, preferred_element_type=jnp.float32)
            total = total + lax.optimization_barrier(jnp.sum(flat * mixed, axis=0)).reshape(fields.shape[2:])
        return total
    summed = lax.map(one_plane, jnp.arange(fields.shape[1], dtype=jnp.int32))
    return conductivity * summed
```

```python
import functools

import jax
import jax.numpy as jnp
from jax import lax
from jax.experimental import pallas as pl
from jax.experimental.pallas import tpu as pltpu
from jax.sharding import PartitionSpec as P

VMEM = 40 * 1024 * 1024
PAIR_STEP = 2048


def column(row):
    count = row.shape[1]
    own = lax.broadcasted_iota(jnp.int32, (count, count), 0) == lax.broadcasted_iota(jnp.int32, (count, count), 1)
    return jnp.sum(jnp.where(own, jnp.broadcast_to(row, (count, count)), 0.0), axis=1, keepdims=True)


def fields_kernel(nz, z_first_ref, positions_ref, block_ref, above_ref, out_ref):
    target = pl.program_id(0)
    places = positions_ref[...].astype(jnp.float32)
    x_place, z_place, y_place = (column(places[axis : axis + 1]) for axis in range(3))
    count, width = block_ref.shape[0], block_ref.shape[2]
    planes = block_ref.shape[1] // nz
    y_gap = lax.broadcasted_iota(jnp.int32, (count, width), 1).astype(jnp.float32) - y_place
    y_part = y_gap * y_gap + 0.5
    z_parts = []
    for z in range(nz):
        z_gap = (z_first_ref[0] + z).astype(jnp.float32) - z_place
        z_parts.append(z_gap * z_gap + y_part)

    def plane_pair(source_ref, row, x_first, keep):
        pair = source_ref[:, row : row + 2 * nz, :].astype(jnp.float32)
        turned = jnp.swapaxes(pair, 0, 1)
        for step in range(keep):
            x_gap = (x_first + step).astype(jnp.float32) - x_place
            x_part = x_gap * x_gap
            for z in range(nz):
                value = turned[step * nz + z] + 4.0 * lax.rsqrt(z_parts[z] + x_part)
                yield step, z, value.astype(jnp.bfloat16)

    for first in range(0, planes, 2):
        for step, z, value in plane_pair(block_ref, first * nz, target * planes + first, 2):
            out_ref[0, first + step, z] = value
    last = target == pl.num_programs(0) - 1
    for _, z, value in plane_pair(above_ref, 0, target * planes + planes, 1):
        out_ref[0, planes, z] = jnp.where(last, jnp.zeros_like(value), value)


def spread_fields(secondary, positions, z_first, groups):
    count, nx, nz, ny = secondary.shape
    planes = nx // groups
    rows = secondary.reshape(count, nx * nz, ny)
    halo_rows = 16
    return pl.pallas_call(
        functools.partial(fields_kernel, nz),
        grid=(groups,),
        in_specs=[
            pl.BlockSpec(memory_space=pltpu.SMEM),
            pl.BlockSpec(positions.shape, lambda i: (0, 0)),
            pl.BlockSpec((count, planes * nz, ny), lambda i: (0, i, 0)),
            pl.BlockSpec(
                (count, halo_rows, ny),
                lambda i: (0, jnp.minimum(i + 1, groups - 1) * (planes * nz // halo_rows), 0),
            ),
        ],
        out_specs=pl.BlockSpec((1, planes + 1, nz, count, ny), lambda i: (i, 0, 0, 0, 0)),
        out_shape=jax.ShapeDtypeStruct((groups, planes + 1, nz, count, ny), jnp.bfloat16),
        compiler_params=pltpu.CompilerParams(vmem_limit_bytes=VMEM),
        name="fields",
    )(z_first, positions, rows, rows)


def pairs_kernel(count, pairs_ref, weights_ref, out_ref, total_ref):
    total_ref[...] = jnp.zeros_like(total_ref)
    ids = lax.broadcasted_iota(jnp.int32, (count, PAIR_STEP), 0)

    @pl.loop(0, pairs_ref.shape[1] // PAIR_STEP)
    def _(step):
        part = pl.ds(pl.multiple_of(step * PAIR_STEP, PAIR_STEP), PAIR_STEP)
        weight = weights_ref[:, part]
        high = weight.astype(jnp.bfloat16).astype(jnp.float32)
        rest = weight - high
        middle = rest.astype(jnp.bfloat16).astype(jnp.float32)
        low = rest - middle
        source = ids == pairs_ref[0:1, part]
        target = jnp.where(ids == pairs_ref[1:2, part], 1.0, 0.0).astype(jnp.bfloat16)
        for term in (high, middle, low):
            hot = jnp.where(source, term, 0.0).astype(jnp.bfloat16)
            total_ref[...] += lax.dot_general(
                hot, target, (((1,), (1,)), ((), ())), preferred_element_type=jnp.float32
            )

    out_ref[...] = total_ref[...].astype(jnp.bfloat16)


def pair_matrix(pairs, weights, count):
    return pl.pallas_call(
        functools.partial(pairs_kernel, count),
        out_shape=jax.ShapeDtypeStruct((count, count), jnp.bfloat16),
        scratch_shapes=[pltpu.VMEM((count, count), jnp.float32)],
        compiler_params=pltpu.CompilerParams(vmem_limit_bytes=VMEM),
        cost_estimate=pl.CostEstimate(
            flops=6 * pairs.shape[0] * count * count, bytes_accessed=12 * pairs.shape[0], transcendentals=0
        ),
        name="pair_weights",
    )(pairs.T, weights.reshape(1, -1))


def form(matrix, slopes):
    total = None
    for slope in slopes:
        mixed = jnp.dot(matrix, slope, preferred_element_type=jnp.float32)
        term = slope.astype(jnp.float32) * mixed
        total = term if total is None else total + term
    return jnp.sum(total, axis=0)


def inner_kernel(fields_ref, matrix_ref, out_ref):
    groups, planes, nz, part, ny = fields_ref.shape
    count = groups * part
    matrix = matrix_ref[...]

    def field(x, z):
        return fields_ref[:, x, z].reshape(count, ny)

    @pl.loop(0, planes - 1)
    def _(x):
        for z in range(nz):
            here = field(x, z)
            ahead = jnp.concatenate([here[:, 1:], jnp.zeros((count, 1), here.dtype)], axis=1)
            slopes = [field(x + 1, z) - here, ahead - here]
            if z < nz - 1:
                slopes.append(field(x, z + 1) - here)
            out_ref[x, z] = form(matrix, slopes)


def outer_kernel(fields_ref, above_ref, matrix_ref, inner_ref, conductivity_ref, out_ref):
    groups, planes, part, ny = above_ref.shape
    count = groups * part
    top = inner_ref.shape[1] - 1
    matrix = matrix_ref[...]
    for x in range(planes):
        slope = above_ref[:, x].reshape(count, ny) - fields_ref[:, x].reshape(count, ny)
        rise = form(matrix, [slope])
        for z in range(top):
            out_ref[x, z] = conductivity_ref[x, z] * inner_ref[x, z]
        out_ref[x, top] = conductivity_ref[x, top] * (inner_ref[x, top] + rise)


def body(secondary, conductivity, positions, pairs, weights):
    groups = lax.axis_size("elec")
    slabs = lax.axis_size("slab")
    nz = secondary.shape[2]
    count = secondary.shape[0] * groups
    z_first = (lax.axis_index("slab") * nz).reshape(1)
    sent = spread_fields(secondary, positions, z_first, groups)
    fields = lax.all_to_all(sent, "elec", split_axis=0, concat_axis=0, tiled=True)
    matrix = pair_matrix(pairs, weights, count)
    planes = fields.shape[1] - 1
    above = lax.ppermute(fields[:, :planes, 0], "slab", [(i + 1, i) for i in range(slabs - 1)])
    params = pltpu.CompilerParams(vmem_limit_bytes=VMEM)
    inner = pl.pallas_call(
        inner_kernel,
        out_shape=jax.ShapeDtypeStruct(conductivity.shape, jnp.float32),
        compiler_params=params,
        cost_estimate=pl.CostEstimate(flops=1600000000, bytes_accessed=3000000, transcendentals=0),
        name="inner_slopes",
    )(fields, matrix)
    return pl.pallas_call(
        outer_kernel,
        out_shape=jax.ShapeDtypeStruct(conductivity.shape, jnp.float32),
        compiler_params=params,
        name="outer_slopes",
    )(fields[:, :planes, nz - 1], above, matrix, inner, conductivity)


def solution(mesh):
    return jax.shard_map(
        body,
        mesh=mesh,
        in_specs=(
            P("elec", None, "slab", None),
            P("elec", "slab", None),
            P(None, "elec"),
            P(),
            P(),
        ),
        out_specs=P("elec", "slab", None),
        check_vma=False,
    )
```

```python
import functools

import jax
import jax.numpy as jnp
from jax import lax
from jax.experimental import pallas as pl
from jax.experimental.pallas import tpu as pltpu
from jax.sharding import PartitionSpec as P

VMEM = 40 * 1024 * 1024
PAIR_STEP = 2048
HALO_ROWS = 16
OFFSETS = [(0, 0), (0, 1), (2, 0), (2, 1), (1, 1), (3, 0), (3, 1), (1, 0)]


def partner(me, offset, groups):
    y_step, flip = offset
    return (me // 2 + y_step) % (groups // 2) * 2 + (me % 2 + flip) % 2


def origin(me, offset, groups):
    return partner(me, ((groups // 2 - offset[0]) % (groups // 2), offset[1]), groups)


def column(row):
    count = row.shape[1]
    own = lax.broadcasted_iota(jnp.int32, (count, count), 0) == lax.broadcasted_iota(jnp.int32, (count, count), 1)
    return jnp.sum(jnp.where(own, jnp.broadcast_to(row, (count, count)), 0.0), axis=1, keepdims=True)


def fields_kernel(offsets, groups, nz, place_ref, positions_ref, rows_ref, *refs):
    outs, (block_ref, halo_ref, block_sem, halo_sem) = refs[:-4], refs[-4:]
    me, z_first = place_ref[0], place_ref[1] * nz
    count, width = rows_ref.shape[0], rows_ref.shape[2]
    total = rows_ref.shape[1]
    planes = total // nz // groups
    targets = [partner(me, offset, groups) for offset in offsets]
    copies = []
    for slot, target in enumerate(targets):
        first = pl.multiple_of(target * (planes * nz), planes * nz)
        after = pl.multiple_of(jnp.minimum(first + planes * nz, total - HALO_ROWS), HALO_ROWS)
        copies.append((
            pltpu.make_async_copy(
                rows_ref.at[:, pl.ds(first, planes * nz), :], block_ref.at[slot], block_sem.at[slot]
            ),
            pltpu.make_async_copy(
                rows_ref.at[:, pl.ds(after, HALO_ROWS), :], halo_ref.at[slot], halo_sem.at[slot]
            ),
        ))
        for copy in copies[-1]:
            copy.start()

    places = positions_ref[...].astype(jnp.float32)
    x_place, z_place, y_place = (column(places[axis : axis + 1]) for axis in range(3))
    y_gap = lax.broadcasted_iota(jnp.int32, (count, width), 1).astype(jnp.float32) - y_place
    y_part = y_gap * y_gap + 0.5
    z_parts = []
    for z in range(nz):
        z_gap = (z_first + z).astype(jnp.float32) - z_place
        z_parts.append(z_gap * z_gap + y_part)

    def planes_of(pair, x_first, keep):
        turned = jnp.swapaxes(pair.astype(jnp.float32), 0, 1)
        for step in range(keep):
            x_gap = (x_first + step).astype(jnp.float32) - x_place
            x_part = x_gap * x_gap
            for z in range(nz):
                value = turned[step * nz + z] + 4.0 * lax.rsqrt(z_parts[z] + x_part)
                yield step, z, value.astype(jnp.bfloat16)

    for slot, target in enumerate(targets):
        out_ref = outs[slot]
        copies[slot][0].wait()
        for first in range(0, planes, 2):
            pair = block_ref[slot, :, first * nz : (first + 2) * nz, :]
            for step, z, value in planes_of(pair, target * planes + first, 2):
                out_ref[z, first + step] = value
        copies[slot][1].wait()
        last = target == groups - 1
        for _, z, value in planes_of(halo_ref[slot, :, : 2 * nz, :], (target + 1) * planes, 1):
            out_ref[z, planes] = jnp.where(last, jnp.zeros_like(value), value)


def spread_fields(offsets, place, secondary, positions, groups):
    count, nx, nz, ny = secondary.shape
    planes = nx // groups
    slots = len(offsets)
    rows = secondary.reshape(count, nx * nz, ny)
    return pl.pallas_call(
        functools.partial(fields_kernel, offsets, groups, nz),
        in_specs=[
            pl.BlockSpec(memory_space=pltpu.SMEM),
            pl.BlockSpec(memory_space=pltpu.VMEM),
            pl.BlockSpec(memory_space=pl.ANY),
        ],
        out_specs=[pl.BlockSpec(memory_space=pltpu.VMEM)] * slots,
        out_shape=[jax.ShapeDtypeStruct((nz, planes + 1, count, ny), jnp.bfloat16)] * slots,
        scratch_shapes=[
            pltpu.VMEM((slots, count, planes * nz, ny), jnp.bfloat16),
            pltpu.VMEM((slots, count, HALO_ROWS, ny), jnp.bfloat16),
            pltpu.SemaphoreType.DMA((slots,)),
            pltpu.SemaphoreType.DMA((slots,)),
        ],
        compiler_params=pltpu.CompilerParams(vmem_limit_bytes=VMEM),
        name="fields",
    )(place, positions, rows)


def pairs_kernel(groups, count, place_ref, pairs_ref, weights_ref, out_ref, total_ref):
    total_ref[...] = jnp.zeros_like(total_ref)
    part = count // groups
    ids = []
    for offset in OFFSETS:
        first = origin(place_ref[0], offset, groups) * part
        ids.append(lax.broadcasted_iota(jnp.int32, (part, PAIR_STEP), 0) + first)
    ids = jnp.concatenate(ids, axis=0)

    @pl.loop(0, pairs_ref.shape[1] // PAIR_STEP)
    def _(step):
        span = pl.ds(pl.multiple_of(step * PAIR_STEP, PAIR_STEP), PAIR_STEP)
        weight = weights_ref[:, span]
        high = weight.astype(jnp.bfloat16).astype(jnp.float32)
        source = ids == pairs_ref[0:1, span]
        target = jnp.where(ids == pairs_ref[1:2, span], 1.0, 0.0).astype(jnp.bfloat16)
        for term in (high, weight - high):
            hot = jnp.where(source, term, 0.0).astype(jnp.bfloat16)
            total_ref[...] += lax.dot_general(
                hot, target, (((1,), (1,)), ((), ())), preferred_element_type=jnp.float32
            )

    out_ref[...] = total_ref[...].astype(jnp.bfloat16)


def pair_matrix(place, pairs, weights, count, groups):
    return pl.pallas_call(
        functools.partial(pairs_kernel, groups, count),
        in_specs=[
            pl.BlockSpec(memory_space=pltpu.SMEM),
            pl.BlockSpec(memory_space=pltpu.VMEM),
            pl.BlockSpec(memory_space=pltpu.VMEM),
        ],
        out_shape=jax.ShapeDtypeStruct((count, count), jnp.bfloat16),
        scratch_shapes=[pltpu.VMEM((count, count), jnp.float32)],
        compiler_params=pltpu.CompilerParams(vmem_limit_bytes=VMEM),
        cost_estimate=pl.CostEstimate(
            flops=4 * pairs.shape[0] * count * count, bytes_accessed=12 * pairs.shape[0], transcendentals=0
        ),
        name="pair_weights",
    )(place, pairs.T, weights.reshape(1, -1))


def form(matrix, slopes):
    total = None
    for slope in slopes:
        mixed = jnp.dot(matrix, slope, preferred_element_type=jnp.float32)
        term = slope.astype(jnp.float32) * mixed
        total = term if total is None else total + term
    return jnp.sum(total, axis=0)


def inner_kernel(matrix_ref, *refs):
    blocks, out_ref = refs[:-1], refs[-1]
    nz, planes, _, ny = blocks[0].shape
    matrix = matrix_ref[...]
    count = matrix.shape[0]

    def field(x, z):
        return jnp.concatenate([block[z, x] for block in blocks], axis=0)

    @pl.loop(0, planes - 1)
    def _(x):
        for z in range(nz):
            here = field(x, z)
            ahead = jnp.concatenate([here[:, 1:], jnp.zeros((count, 1), here.dtype)], axis=1)
            slopes = [field(x + 1, z) - here, ahead - here]
            if z < nz - 1:
                slopes.append(field(x, z + 1) - here)
            out_ref[x, z] = form(matrix, slopes)


def outer_kernel(matrix_ref, inner_ref, conductivity_ref, above_ref, *refs):
    blocks, out_ref = refs[:-1], refs[-1]
    planes = above_ref.shape[1]
    top = blocks[0].shape[0] - 1
    matrix = matrix_ref[...]
    for x in range(planes):
        here = jnp.concatenate([block[top, x] for block in blocks], axis=0)
        slope = above_ref[:, x].reshape(here.shape) - here
        rise = form(matrix, [slope])
        for z in range(top):
            out_ref[x, z] = conductivity_ref[x, z] * inner_ref[x, z]
        out_ref[x, top] = conductivity_ref[x, top] * (inner_ref[x, top] + rise)


def body(secondary, conductivity, positions, pairs, weights):
    groups = lax.axis_size("elec")
    slabs = lax.axis_size("slab")
    count = secondary.shape[0] * groups
    place = jnp.stack([lax.axis_index("elec"), lax.axis_index("slab")])
    blocks = spread_fields(OFFSETS, place, secondary, positions, groups)
    planes = blocks[0].shape[1] - 1
    blocks = [blocks[0]] + [
        lax.ppermute(block, "elec", [(i, partner(i, offset, groups)) for i in range(groups)])
        for block, offset in zip(blocks[1:], OFFSETS[1:])
    ]
    matrix = pair_matrix(place, pairs, weights, count, groups)
    plane = jnp.stack([block[0, :planes] for block in blocks])
    plane, matrix = lax.optimization_barrier((plane, matrix))
    above = lax.ppermute(plane, "slab", [(i + 1, i) for i in range(slabs - 1)])
    params = pltpu.CompilerParams(vmem_limit_bytes=VMEM)
    inner = pl.pallas_call(
        inner_kernel,
        out_shape=jax.ShapeDtypeStruct(conductivity.shape, jnp.float32),
        compiler_params=params,
        cost_estimate=pl.CostEstimate(flops=1600000000, bytes_accessed=3000000, transcendentals=0),
        name="inner_slopes",
    )(matrix, *blocks)
    return pl.pallas_call(
        outer_kernel,
        out_shape=jax.ShapeDtypeStruct(conductivity.shape, jnp.float32),
        compiler_params=params,
        name="outer_slopes",
    )(matrix, inner, conductivity, above, *blocks)


def solution(mesh):
    return jax.shard_map(
        body,
        mesh=mesh,
        in_specs=(
            P("elec", None, "slab", None),
            P("elec", "slab", None),
            P(None, "elec"),
            P(),
            P(),
        ),
        out_specs=P("elec", "slab", None),
        check_vma=False,
    )
```

```python
import functools

import jax
import jax.numpy as jnp
from jax import lax
from jax.experimental import pallas as pl
from jax.experimental.pallas import tpu as pltpu
from jax.sharding import PartitionSpec as P

VMEM = 40 * 1024 * 1024
PAIR_STEP = 2048
HALO_ROWS = 16
EARLY = 6
OFFSETS = [(0, 0), (0, 1), (2, 0), (2, 1), (1, 1), (3, 0), (3, 1), (1, 0)]


def partner(me, offset, groups):
    y_step, flip = offset
    return (me // 2 + y_step) % (groups // 2) * 2 + (me % 2 + flip) % 2


def origin(me, offset, groups):
    return partner(me, ((groups // 2 - offset[0]) % (groups // 2), offset[1]), groups)


def column(row):
    count = row.shape[1]
    own = lax.broadcasted_iota(jnp.int32, (count, count), 0) == lax.broadcasted_iota(jnp.int32, (count, count), 1)
    return jnp.sum(jnp.where(own, jnp.broadcast_to(row, (count, count)), 0.0), axis=1, keepdims=True)


def fields_kernel(offsets, groups, nz, place_ref, positions_ref, rows_ref, *refs):
    outs = refs
    me, z_first = place_ref[0], place_ref[1] * nz
    count, width = rows_ref.shape[0], rows_ref.shape[2]
    total = rows_ref.shape[1]
    planes = total // nz // groups
    targets = [partner(me, offset, groups) for offset in offsets]

    places = positions_ref[...].astype(jnp.float32)
    x_place, z_place, y_place = (column(places[axis : axis + 1]) for axis in range(3))
    y_gap = lax.broadcasted_iota(jnp.int32, (count, width), 1).astype(jnp.float32) - y_place
    y_part = y_gap * y_gap + 0.5
    z_parts = []
    for z in range(nz):
        z_gap = (z_first + z).astype(jnp.float32) - z_place
        z_parts.append(z_gap * z_gap + y_part)

    def planes_of(pair, x_first, keep):
        turned = jnp.swapaxes(pair.astype(jnp.float32), 0, 1)
        for step in range(keep):
            x_gap = (x_first + step).astype(jnp.float32) - x_place
            x_part = x_gap * x_gap
            for z in range(nz):
                value = turned[step * nz + z] + 4.0 * lax.rsqrt(z_parts[z] + x_part)
                yield step, z, value.astype(jnp.bfloat16)

    for slot, target in enumerate(targets):
        out_ref = outs[slot]
        start = pl.multiple_of(target * (planes * nz), planes * nz)
        after = pl.multiple_of(jnp.minimum(start + planes * nz, total - HALO_ROWS), HALO_ROWS)
        for first in range(0, planes, 2):
            pair = rows_ref[:, pl.ds(start + first * nz, 2 * nz), :]
            for step, z, value in planes_of(pair, target * planes + first, 2):
                out_ref[z, first + step] = value
        last = target == groups - 1
        for _, z, value in planes_of(rows_ref[:, pl.ds(after, 2 * nz), :], (target + 1) * planes, 1):
            out_ref[z, planes] = jnp.where(last, jnp.zeros_like(value), value)


def spread_fields(offsets, place, secondary, positions, groups):
    count, nx, nz, ny = secondary.shape
    planes = nx // groups
    slots = len(offsets)
    rows = secondary.reshape(count, nx * nz, ny)
    return pl.pallas_call(
        functools.partial(fields_kernel, offsets, groups, nz),
        in_specs=[
            pl.BlockSpec(memory_space=pltpu.SMEM),
            pl.BlockSpec(memory_space=pltpu.VMEM),
            pl.BlockSpec(memory_space=pltpu.VMEM),
        ],
        out_specs=[pl.BlockSpec(memory_space=pltpu.VMEM)] * slots,
        out_shape=[jax.ShapeDtypeStruct((nz, planes + 1, count, ny), jnp.bfloat16)] * slots,
        compiler_params=pltpu.CompilerParams(vmem_limit_bytes=VMEM),
        name="fields",
    )(place, positions, rows)


def pairs_kernel(groups, count, place_ref, pairs_ref, weights_ref, out_ref, both_ref, total_ref):
    total_ref[...] = jnp.zeros_like(total_ref)
    part = count // groups
    ids = []
    for offset in OFFSETS:
        first = origin(place_ref[0], offset, groups) * part
        ids.append(lax.broadcasted_iota(jnp.int32, (part, PAIR_STEP), 0) + first)
    ids = jnp.concatenate(ids, axis=0)

    @pl.loop(0, pairs_ref.shape[1] // PAIR_STEP)
    def _(step):
        span = pl.ds(pl.multiple_of(step * PAIR_STEP, PAIR_STEP), PAIR_STEP)
        weight = weights_ref[:, span]
        high = weight.astype(jnp.bfloat16).astype(jnp.float32)
        source = ids == pairs_ref[0:1, span]
        target = jnp.where(ids == pairs_ref[1:2, span], 1.0, 0.0).astype(jnp.bfloat16)
        for term in (high, weight - high):
            hot = jnp.where(source, term, 0.0).astype(jnp.bfloat16)
            total_ref[...] += lax.dot_general(
                hot, target, (((1,), (1,)), ((), ())), preferred_element_type=jnp.float32
            )

    out_ref[...] = total_ref[...].astype(jnp.bfloat16)
    both_ref[...] = (total_ref[...] + jnp.transpose(total_ref[...])).astype(jnp.bfloat16)


def pair_matrix(place, pairs, weights, count, groups):
    return pl.pallas_call(
        functools.partial(pairs_kernel, groups, count),
        in_specs=[
            pl.BlockSpec(memory_space=pltpu.SMEM),
            pl.BlockSpec(memory_space=pltpu.VMEM),
            pl.BlockSpec(memory_space=pltpu.VMEM),
        ],
        out_shape=[jax.ShapeDtypeStruct((count, count), jnp.bfloat16)] * 2,
        scratch_shapes=[pltpu.VMEM((count, count), jnp.float32)],
        compiler_params=pltpu.CompilerParams(vmem_limit_bytes=VMEM),
        cost_estimate=pl.CostEstimate(
            flops=4 * pairs.shape[0] * count * count, bytes_accessed=12 * pairs.shape[0], transcendentals=0
        ),
        name="pair_weights",
    )(place, pairs.T, weights.reshape(1, -1))


def form(matrix, slopes):
    total = None
    for slope in slopes:
        mixed = jnp.dot(matrix, slope, preferred_element_type=jnp.float32)
        term = slope.astype(jnp.float32) * mixed
        total = term if total is None else total + term
    return jnp.sum(total, axis=0)


def node_slopes(blocks, x, z):
    nz = blocks[0].shape[0]

    def field(x, z):
        return jnp.concatenate([block[z, x] for block in blocks], axis=0)

    here = field(x, z)
    ahead = jnp.concatenate([here[:, 1:], jnp.zeros((here.shape[0], 1), here.dtype)], axis=1)
    slopes = [field(x + 1, z) - here, ahead - here]
    if z < nz - 1:
        slopes.append(field(x, z + 1) - here)
    return slopes


def early_kernel(matrix_ref, *refs):
    blocks, out_ref = refs[:-1], refs[-1]
    nz, planes, part, _ = blocks[0].shape
    count = part * len(blocks)
    matrix = matrix_ref[:count, :count]

    @pl.loop(0, planes - 1)
    def _(x):
        for z in range(nz):
            out_ref[x, z] = form(matrix, node_slopes(blocks, x, z))


def late_kernel(early, matrix_ref, both_ref, early_ref, *refs):
    blocks, out_ref = refs[:-1], refs[-1]
    nz, planes, part, _ = blocks[0].shape
    first = early * part
    matrix = jnp.concatenate([both_ref[first:, :first], matrix_ref[first:, first:]], axis=1)

    @pl.loop(0, planes - 1)
    def _(x):
        for z in range(nz):
            total = None
            for slope in node_slopes(blocks, x, z):
                mixed = jnp.dot(matrix, slope, preferred_element_type=jnp.float32)
                term = slope[first:].astype(jnp.float32) * mixed
                total = term if total is None else total + term
            out_ref[x, z] = early_ref[x, z] + jnp.sum(total, axis=0)


def outer_kernel(matrix_ref, inner_ref, conductivity_ref, early_ref, late_ref, *refs):
    blocks, out_ref = refs[:-1], refs[-1]
    planes = early_ref.shape[1]
    top = blocks[0].shape[0] - 1
    matrix = matrix_ref[...]
    for x in range(planes):
        here = jnp.concatenate([block[top, x] for block in blocks], axis=0)
        above = jnp.concatenate([early_ref[:, x], late_ref[:, x]], axis=0).reshape(here.shape)
        slope = above - here
        rise = form(matrix, [slope])
        for z in range(top):
            out_ref[x, z] = conductivity_ref[x, z] * inner_ref[x, z]
        out_ref[x, top] = conductivity_ref[x, top] * (inner_ref[x, top] + rise)


def body(secondary, conductivity, positions, pairs, weights):
    groups = lax.axis_size("elec")
    slabs = lax.axis_size("slab")
    count = secondary.shape[0] * groups
    place = jnp.stack([lax.axis_index("elec"), lax.axis_index("slab")])
    blocks = spread_fields(OFFSETS, place, secondary, positions.astype(jnp.float32), groups)
    planes = blocks[0].shape[1] - 1
    blocks = [blocks[0]] + [
        lax.ppermute(block, "elec", [(i, partner(i, offset, groups)) for i in range(groups)])
        for block, offset in zip(blocks[1:], OFFSETS[1:])
    ]
    matrix, both = pair_matrix(place, pairs, weights, count, groups)
    params = pltpu.CompilerParams(vmem_limit_bytes=VMEM)
    result = jax.ShapeDtypeStruct(conductivity.shape, jnp.float32)

    def lowest(some):
        plane = jnp.stack([block[0, :planes] for block in some])
        return lax.ppermute(plane, "slab", [(i + 1, i) for i in range(slabs - 1)])

    some = lax.optimization_barrier((*blocks[:EARLY], matrix))
    above = [lowest(some[:-1])]
    early = pl.pallas_call(
        early_kernel,
        out_shape=result,
        compiler_params=params,
        cost_estimate=pl.CostEstimate(flops=900000000, bytes_accessed=3000000, transcendentals=0),
        name="early_slopes",
    )(matrix, *blocks[:EARLY])
    rest, early = lax.optimization_barrier((tuple(blocks[EARLY:]), early))
    above.append(lowest(rest))
    inner = pl.pallas_call(
        functools.partial(late_kernel, EARLY),
        out_shape=result,
        compiler_params=params,
        cost_estimate=pl.CostEstimate(flops=700000000, bytes_accessed=3000000, transcendentals=0),
        name="late_slopes",
    )(matrix, both, early, *blocks)
    return pl.pallas_call(
        outer_kernel,
        out_shape=result,
        compiler_params=params,
        name="outer_slopes",
    )(matrix, inner, conductivity, *above, *blocks)


def solution(mesh):
    return jax.shard_map(
        body,
        mesh=mesh,
        in_specs=(
            P("elec", None, "slab", None),
            P("elec", "slab", None),
            P(None, "elec"),
            P(),
            P(),
        ),
        out_specs=P("elec", "slab", None),
        check_vma=False,
    )
```

```python
import functools

import jax
import jax.numpy as jnp
from jax import lax
from jax.experimental import pallas as pl
from jax.experimental.pallas import tpu as pltpu
from jax.sharding import PartitionSpec as P

VMEM = 40 * 1024 * 1024
PAIR_STEP = 4096
HALO_ROWS = 16
EARLY = 6
OFFSETS = [(0, 0), (0, 1), (2, 0), (2, 1), (1, 1), (3, 0), (3, 1), (1, 0)]


def partner(me, offset, groups):
    y_step, flip = offset
    return (me // 2 + y_step) % (groups // 2) * 2 + (me % 2 + flip) % 2


def origin(me, offset, groups):
    return partner(me, ((groups // 2 - offset[0]) % (groups // 2), offset[1]), groups)


def column(row):
    count = row.shape[1]
    own = lax.broadcasted_iota(jnp.int32, (count, count), 0) == lax.broadcasted_iota(jnp.int32, (count, count), 1)
    return jnp.sum(jnp.where(own, jnp.broadcast_to(row, (count, count)), 0.0), axis=1, keepdims=True)


def fields_kernel(offsets, groups, nz, place_ref, positions_ref, rows_ref, *refs):
    outs = refs
    me, z_first = place_ref[0], place_ref[1] * nz
    count, width = rows_ref.shape[0], rows_ref.shape[2]
    total = rows_ref.shape[1]
    planes = total // nz // groups
    targets = [partner(me, offset, groups) for offset in offsets]

    places = positions_ref[...].astype(jnp.float32)
    x_place, z_place, y_place = (column(places[axis : axis + 1]) for axis in range(3))
    y_gap = lax.broadcasted_iota(jnp.int32, (count, width), 1).astype(jnp.float32) - y_place
    y_part = y_gap * y_gap + 0.5
    z_parts = []
    for z in range(nz):
        z_gap = (z_first + z).astype(jnp.float32) - z_place
        z_parts.append(z_gap * z_gap + y_part)

    def planes_of(pair, x_first, keep):
        turned = jnp.swapaxes(pair.astype(jnp.float32), 0, 1)
        for step in range(keep):
            x_gap = (x_first + step).astype(jnp.float32) - x_place
            x_part = x_gap * x_gap
            for z in range(nz):
                value = turned[step * nz + z] + 4.0 * lax.rsqrt(z_parts[z] + x_part)
                yield step, z, value.astype(jnp.bfloat16)

    for slot, target in enumerate(targets):
        out_ref = outs[slot]
        start = pl.multiple_of(target * (planes * nz), planes * nz)
        after = pl.multiple_of(jnp.minimum(start + planes * nz, total - HALO_ROWS), HALO_ROWS)
        for first in range(0, planes, 2):
            pair = rows_ref[:, pl.ds(start + first * nz, 2 * nz), :]
            for step, z, value in planes_of(pair, target * planes + first, 2):
                out_ref[z, first + step] = value
        last = target == groups - 1
        for _, z, value in planes_of(rows_ref[:, pl.ds(after, 2 * nz), :], (target + 1) * planes, 1):
            out_ref[z, planes] = jnp.where(last, jnp.zeros_like(value), value)


def spread_fields(offsets, place, secondary, positions, groups):
    count, nx, nz, ny = secondary.shape
    planes = nx // groups
    slots = len(offsets)
    rows = secondary.reshape(count, nx * nz, ny)
    return pl.pallas_call(
        functools.partial(fields_kernel, offsets, groups, nz),
        in_specs=[
            pl.BlockSpec(memory_space=pltpu.SMEM),
            pl.BlockSpec(memory_space=pltpu.VMEM),
            pl.BlockSpec(memory_space=pltpu.VMEM),
        ],
        out_specs=[pl.BlockSpec(memory_space=pltpu.VMEM)] * slots,
        out_shape=[jax.ShapeDtypeStruct((nz, planes + 1, count, ny), jnp.bfloat16)] * slots,
        compiler_params=pltpu.CompilerParams(vmem_limit_bytes=VMEM),
        name="fields",
    )(place, positions, rows)


def pairs_kernel(groups, count, place_ref, pairs_ref, weights_ref, out_ref, both_ref, total_ref):
    total_ref[...] = jnp.zeros_like(total_ref)
    part = count // groups
    ids = []
    for offset in OFFSETS:
        first = origin(place_ref[0], offset, groups) * part
        ids.append(lax.broadcasted_iota(jnp.int32, (part, PAIR_STEP), 0) + first)
    ids = jnp.concatenate(ids, axis=0)

    @pl.loop(0, pairs_ref.shape[1] // PAIR_STEP)
    def _(step):
        span = pl.ds(pl.multiple_of(step * PAIR_STEP, PAIR_STEP), PAIR_STEP)
        weight = weights_ref[:, span]
        high = weight.astype(jnp.bfloat16).astype(jnp.float32)
        source = ids == pairs_ref[0:1, span]
        target = jnp.where(ids == pairs_ref[1:2, span], 1.0, 0.0).astype(jnp.bfloat16)
        for term in (high, weight - high):
            hot = jnp.where(source, term, 0.0).astype(jnp.bfloat16)
            total_ref[...] += lax.dot_general(
                hot, target, (((1,), (1,)), ((), ())), preferred_element_type=jnp.float32
            )

    out_ref[...] = total_ref[...].astype(jnp.bfloat16)
    both_ref[...] = (total_ref[...] + jnp.transpose(total_ref[...])).astype(jnp.bfloat16)


def pair_matrix(place, pairs, weights, count, groups):
    return pl.pallas_call(
        functools.partial(pairs_kernel, groups, count),
        in_specs=[
            pl.BlockSpec(memory_space=pltpu.SMEM),
            pl.BlockSpec(memory_space=pltpu.VMEM),
            pl.BlockSpec(memory_space=pltpu.VMEM),
        ],
        out_shape=[jax.ShapeDtypeStruct((count, count), jnp.bfloat16)] * 2,
        scratch_shapes=[pltpu.VMEM((count, count), jnp.float32)],
        compiler_params=pltpu.CompilerParams(vmem_limit_bytes=VMEM),
        cost_estimate=pl.CostEstimate(
            flops=4 * pairs.shape[0] * count * count, bytes_accessed=12 * pairs.shape[0], transcendentals=0
        ),
        name="pair_weights",
    )(place, pairs.T, weights.reshape(1, -1))


def forms(matrix, slopes, first=0):
    flat = [(key, slope) for key, some in slopes.items() for slope in some]
    totals = {}
    for at in range(0, len(flat), 2):
        pair = flat[at : at + 2]
        width = pair[0][1].shape[1]
        mixed = jnp.dot(
            matrix, jnp.concatenate([slope for _, slope in pair], axis=1), preferred_element_type=jnp.float32
        )
        for index, (key, slope) in enumerate(pair):
            term = slope[first:].astype(jnp.float32) * mixed[:, index * width : (index + 1) * width]
            totals[key] = totals[key] + term if key in totals else term
    return {key: jnp.sum(total, axis=0) for key, total in totals.items()}


def node_slopes(blocks, x, z):
    nz = blocks[0].shape[0]

    def field(x, z):
        return jnp.concatenate([block[z, x] for block in blocks], axis=0)

    here = field(x, z)
    ahead = jnp.concatenate([here[:, 1:], jnp.zeros((here.shape[0], 1), here.dtype)], axis=1)
    slopes = [field(x + 1, z) - here, ahead - here]
    if z < nz - 1:
        slopes.append(field(x, z + 1) - here)
    return slopes


def early_kernel(matrix_ref, *refs):
    blocks, out_ref = refs[:-1], refs[-1]
    nz, planes, part, _ = blocks[0].shape
    count = part * len(blocks)
    matrix = matrix_ref[:count, :count]

    @pl.loop(0, (planes - 1) // 2)
    def _(half):
        nodes = [(2 * half + step, step, z) for step in range(2) for z in range(nz)]
        sums = forms(matrix, {(step, z): node_slopes(blocks, x, z) for x, step, z in nodes})
        for x, step, z in nodes:
            out_ref[x, z] = sums[step, z]


def late_kernel(early, matrix_ref, both_ref, early_ref, *refs):
    blocks, out_ref = refs[:-1], refs[-1]
    nz, planes, part, _ = blocks[0].shape
    first = early * part
    matrix = jnp.concatenate([both_ref[first:, :first], matrix_ref[first:, first:]], axis=1)

    @pl.loop(0, (planes - 1) // 2)
    def _(half):
        nodes = [(2 * half + step, step, z) for step in range(2) for z in range(nz)]
        sums = forms(matrix, {(step, z): node_slopes(blocks, x, z) for x, step, z in nodes}, first)
        for x, step, z in nodes:
            out_ref[x, z] = early_ref[x, z] + sums[step, z]


def outer_kernel(matrix_ref, inner_ref, conductivity_ref, early_ref, late_ref, *refs):
    blocks, out_ref = refs[:-1], refs[-1]
    planes = early_ref.shape[1]
    top = blocks[0].shape[0] - 1
    slopes = {}
    for x in range(planes):
        here = jnp.concatenate([block[top, x] for block in blocks], axis=0)
        above = jnp.concatenate([early_ref[:, x], late_ref[:, x]], axis=0).reshape(here.shape)
        slopes[x] = [above - here]
    rises = forms(matrix_ref[...], slopes)
    for x in range(planes):
        for z in range(top):
            out_ref[x, z] = conductivity_ref[x, z] * inner_ref[x, z]
        out_ref[x, top] = conductivity_ref[x, top] * (inner_ref[x, top] + rises[x])


def body(secondary, conductivity, positions, pairs, weights):
    groups = lax.axis_size("elec")
    slabs = lax.axis_size("slab")
    count = secondary.shape[0] * groups
    place = jnp.stack([lax.axis_index("elec"), lax.axis_index("slab")])
    nodes = positions.astype(jnp.float32)
    blocks = list(spread_fields(OFFSETS[1:], place, secondary, nodes, groups))
    blocks = list(spread_fields(OFFSETS[:1], place, secondary, nodes, groups)) + blocks
    planes = blocks[0].shape[1] - 1
    blocks = [blocks[0]] + [
        lax.ppermute(block, "elec", [(i, partner(i, offset, groups)) for i in range(groups)])
        for block, offset in zip(blocks[1:], OFFSETS[1:])
    ]
    matrix, both = pair_matrix(place, pairs, weights, count, groups)
    params = pltpu.CompilerParams(vmem_limit_bytes=VMEM)
    result = jax.ShapeDtypeStruct(conductivity.shape, jnp.float32)

    def lowest(some):
        plane = jnp.stack([block[0, :planes] for block in some])
        return lax.ppermute(plane, "slab", [(i + 1, i) for i in range(slabs - 1)])

    some = lax.optimization_barrier((*blocks[:EARLY], matrix))
    above = [lowest(some[:-1])]
    early = pl.pallas_call(
        early_kernel,
        out_shape=result,
        compiler_params=params,
        cost_estimate=pl.CostEstimate(flops=900000000, bytes_accessed=3000000, transcendentals=0),
        name="early_slopes",
    )(matrix, *blocks[:EARLY])
    rest, early = lax.optimization_barrier((tuple(blocks[EARLY:]), early))
    above.append(lowest(rest))
    inner = pl.pallas_call(
        functools.partial(late_kernel, EARLY),
        out_shape=result,
        compiler_params=params,
        cost_estimate=pl.CostEstimate(flops=700000000, bytes_accessed=3000000, transcendentals=0),
        name="late_slopes",
    )(matrix, both, early, *blocks)
    return pl.pallas_call(
        outer_kernel,
        out_shape=result,
        compiler_params=params,
        name="outer_slopes",
    )(matrix, inner, conductivity, *above, *blocks)


def solution(mesh):
    return jax.shard_map(
        body,
        mesh=mesh,
        in_specs=(
            P("elec", None, "slab", None),
            P("elec", "slab", None),
            P(None, "elec"),
            P(),
            P(),
        ),
        out_specs=P("elec", "slab", None),
        check_vma=False,
    )
```

```python
import functools

import jax
import jax.numpy as jnp
from jax import lax
from jax.experimental import pallas as pl
from jax.experimental.pallas import tpu as pltpu
from jax.sharding import PartitionSpec as P

VMEM = 40 * 1024 * 1024
PAIR_STEP = 4096
HALO_ROWS = 16
EARLY = 6
OFFSETS = [(0, 0), (0, 1), (2, 0), (2, 1), (1, 1), (3, 0), (3, 1), (1, 0)]


def partner(me, offset, groups):
    y_step, flip = offset
    return (me // 2 + y_step) % (groups // 2) * 2 + (me % 2 + flip) % 2


def origin(me, offset, groups):
    return partner(me, ((groups // 2 - offset[0]) % (groups // 2), offset[1]), groups)


def column(row):
    count = row.shape[1]
    own = lax.broadcasted_iota(jnp.int32, (count, count), 0) == lax.broadcasted_iota(jnp.int32, (count, count), 1)
    return jnp.sum(jnp.where(own, jnp.broadcast_to(row, (count, count)), 0.0), axis=1, keepdims=True)


def fields_kernel(offsets, groups, nz, place_ref, positions_ref, rows_ref, *refs):
    outs = refs
    me, z_first = place_ref[0], place_ref[1] * nz
    count, width = rows_ref.shape[0], rows_ref.shape[2]
    total = rows_ref.shape[1]
    planes = total // nz // groups
    targets = [partner(me, offset, groups) for offset in offsets]

    places = positions_ref[...].astype(jnp.float32)
    x_place, z_place, y_place = (column(places[axis : axis + 1]) for axis in range(3))
    y_gap = lax.broadcasted_iota(jnp.int32, (count, width), 1).astype(jnp.float32) - y_place
    y_part = y_gap * y_gap + 0.5
    z_parts = []
    for z in range(nz):
        z_gap = (z_first + z).astype(jnp.float32) - z_place
        z_parts.append(z_gap * z_gap + y_part)

    def planes_of(pair, x_first, keep):
        turned = jnp.swapaxes(pair.astype(jnp.float32), 0, 1)
        for step in range(keep):
            x_gap = (x_first + step).astype(jnp.float32) - x_place
            x_part = x_gap * x_gap
            for z in range(nz):
                value = turned[step * nz + z] + 4.0 * lax.rsqrt(z_parts[z] + x_part)
                yield step, z, value.astype(jnp.bfloat16)

    for slot, target in enumerate(targets):
        out_ref = outs[slot]
        start = pl.multiple_of(target * (planes * nz), planes * nz)
        after = pl.multiple_of(jnp.minimum(start + planes * nz, total - HALO_ROWS), HALO_ROWS)
        for first in range(0, planes, 2):
            pair = rows_ref[:, pl.ds(start + first * nz, 2 * nz), :]
            for step, z, value in planes_of(pair, target * planes + first, 2):
                out_ref[z, first + step] = value
        last = target == groups - 1
        for _, z, value in planes_of(rows_ref[:, pl.ds(after, 2 * nz), :], (target + 1) * planes, 1):
            out_ref[z, planes] = jnp.where(last, jnp.zeros_like(value), value)


def spread_fields(offsets, place, secondary, positions, groups):
    count, nx, nz, ny = secondary.shape
    planes = nx // groups
    slots = len(offsets)
    rows = secondary.reshape(count, nx * nz, ny)
    return pl.pallas_call(
        functools.partial(fields_kernel, offsets, groups, nz),
        in_specs=[
            pl.BlockSpec(memory_space=pltpu.SMEM),
            pl.BlockSpec(memory_space=pltpu.VMEM),
            pl.BlockSpec(memory_space=pltpu.VMEM),
        ],
        out_specs=[pl.BlockSpec(memory_space=pltpu.VMEM)] * slots,
        out_shape=[jax.ShapeDtypeStruct((nz, planes + 1, count, ny), jnp.bfloat16)] * slots,
        compiler_params=pltpu.CompilerParams(vmem_limit_bytes=VMEM),
        name="fields",
    )(place, positions, rows)


def pairs_kernel(groups, count, place_ref, pairs_ref, weights_ref, out_ref, both_ref, total_ref):
    total_ref[...] = jnp.zeros_like(total_ref)
    part = count // groups
    ids = []
    for offset in OFFSETS:
        first = origin(place_ref[0], offset, groups) * part
        ids.append(lax.broadcasted_iota(jnp.int32, (part, PAIR_STEP), 0) + first)
    ids = jnp.concatenate(ids, axis=0)

    @pl.loop(0, pairs_ref.shape[1] // PAIR_STEP)
    def _(step):
        span = pl.ds(pl.multiple_of(step * PAIR_STEP, PAIR_STEP), PAIR_STEP)
        weight = weights_ref[:, span]
        high = weight.astype(jnp.bfloat16).astype(jnp.float32)
        source = ids == pairs_ref[0:1, span]
        target = jnp.where(ids == pairs_ref[1:2, span], 1.0, 0.0).astype(jnp.bfloat16)
        for term in (high, weight - high):
            hot = jnp.where(source, term, 0.0).astype(jnp.bfloat16)
            total_ref[...] += lax.dot_general(
                hot, target, (((1,), (1,)), ((), ())), preferred_element_type=jnp.float32
            )

    out_ref[...] = total_ref[...].astype(jnp.bfloat16)
    both_ref[...] = (total_ref[...] + jnp.transpose(total_ref[...])).astype(jnp.bfloat16)


def pair_matrix(place, pairs, weights, count, groups):
    return pl.pallas_call(
        functools.partial(pairs_kernel, groups, count),
        in_specs=[
            pl.BlockSpec(memory_space=pltpu.SMEM),
            pl.BlockSpec(memory_space=pltpu.VMEM),
            pl.BlockSpec(memory_space=pltpu.VMEM),
        ],
        out_shape=[jax.ShapeDtypeStruct((count, count), jnp.bfloat16)] * 2,
        scratch_shapes=[pltpu.VMEM((count, count), jnp.float32)],
        compiler_params=pltpu.CompilerParams(vmem_limit_bytes=VMEM),
        cost_estimate=pl.CostEstimate(
            flops=4 * pairs.shape[0] * count * count, bytes_accessed=12 * pairs.shape[0], transcendentals=0
        ),
        name="pair_weights",
    )(place, pairs.T, weights.reshape(1, -1))


def forms(matrix, slopes, first=0):
    flat = [(key, slope) for key, some in slopes.items() for slope in some]
    totals = {}
    for at in range(0, len(flat), 2):
        pair = flat[at : at + 2]
        width = pair[0][1].shape[1]
        mixed = jnp.dot(
            matrix, jnp.concatenate([slope for _, slope in pair], axis=1), preferred_element_type=jnp.float32
        )
        for index, (key, slope) in enumerate(pair):
            term = slope[first:].astype(jnp.float32) * mixed[:, index * width : (index + 1) * width]
            totals[key] = totals[key] + term if key in totals else term
    return {key: jnp.sum(total, axis=0) for key, total in totals.items()}


def node_slopes(blocks, x, z):
    nz = blocks[0].shape[0]

    def field(x, z):
        return jnp.concatenate([block[z, x] for block in blocks], axis=0)

    here = field(x, z)
    ahead = jnp.concatenate([here[:, 1:], jnp.zeros((here.shape[0], 1), here.dtype)], axis=1)
    slopes = [field(x + 1, z) - here, ahead - here]
    if z < nz - 1:
        slopes.append(field(x, z + 1) - here)
    return slopes


def early_kernel(matrix_ref, *refs):
    blocks, out_ref = refs[:-1], refs[-1]
    nz, planes, part, _ = blocks[0].shape
    count = part * len(blocks)
    matrix = matrix_ref[:count, :count]

    @pl.loop(0, (planes - 1) // 2)
    def _(half):
        nodes = [(2 * half + step, step, z) for step in range(2) for z in range(nz)]
        sums = forms(matrix, {(step, z): node_slopes(blocks, x, z) for x, step, z in nodes})
        for x, step, z in nodes:
            out_ref[x, z] = sums[step, z]


def late_kernel(early, matrix_ref, both_ref, early_ref, above_ref, *refs):
    blocks, (out_ref, mixed_ref) = refs[:-2], refs[-2:]
    nz, planes, part, _ = blocks[0].shape
    first = early * part
    matrix = jnp.concatenate([both_ref[first:, :first], matrix_ref[first:, first:]], axis=1)
    rows = jnp.concatenate([matrix_ref[:first, :first], both_ref[first:, :first]], axis=0)

    def rise(x):
        return jnp.concatenate([above_ref[slot, x] - blocks[slot][nz - 1, x] for slot in range(early)], axis=0)

    @pl.loop(0, (planes - 1) // 2)
    def _(half):
        nodes = [(2 * half + step, step, z) for step in range(2) for z in range(nz)]
        sums = forms(matrix, {(step, z): node_slopes(blocks, x, z) for x, step, z in nodes}, first)
        rises = [rise(2 * half + step) for step in range(2)]
        width = rises[0].shape[1]
        mixed = jnp.dot(rows, jnp.concatenate(rises, axis=1), preferred_element_type=jnp.float32)
        for x, step, z in nodes:
            value = early_ref[x, z] + sums[step, z]
            if z == nz - 1:
                own = mixed[:, step * width : (step + 1) * width]
                value += jnp.sum(rises[step].astype(jnp.float32) * own[:first], axis=0)
                mixed_ref[x] = own[first:]
            out_ref[x, z] = value


def outer_kernel(early, matrix_ref, inner_ref, mixed_ref, conductivity_ref, above_ref, *refs):
    blocks, out_ref = refs[:-1], refs[-1]
    planes = above_ref.shape[1]
    top, part = blocks[0].shape[0] - 1, blocks[0].shape[2]
    first = early * part
    matrix = matrix_ref[first:, first:]
    for x in range(0, planes, 2):
        slopes = [
            jnp.concatenate([above_ref[slot, x + step] - block[top, x + step] for slot, block in enumerate(blocks)], axis=0)
            for step in range(2)
        ]
        width = slopes[0].shape[1]
        mixed = jnp.dot(matrix, jnp.concatenate(slopes, axis=1), preferred_element_type=jnp.float32)
        for step in range(2):
            own = mixed_ref[x + step] + mixed[:, step * width : (step + 1) * width]
            rise = jnp.sum(slopes[step].astype(jnp.float32) * own, axis=0)
            for z in range(top):
                out_ref[x + step, z] = conductivity_ref[x + step, z] * inner_ref[x + step, z]
            out_ref[x + step, top] = conductivity_ref[x + step, top] * (inner_ref[x + step, top] + rise)


def body(secondary, conductivity, positions, pairs, weights):
    groups = lax.axis_size("elec")
    slabs = lax.axis_size("slab")
    count = secondary.shape[0] * groups
    place = jnp.stack([lax.axis_index("elec"), lax.axis_index("slab")])
    nodes = positions.astype(jnp.float32)
    blocks = list(spread_fields(OFFSETS[1:], place, secondary, nodes, groups))
    blocks = list(spread_fields(OFFSETS[:1], place, secondary, nodes, groups)) + blocks
    planes = blocks[0].shape[1] - 1
    blocks = [blocks[0]] + [
        lax.ppermute(block, "elec", [(i, partner(i, offset, groups)) for i in range(groups)])
        for block, offset in zip(blocks[1:], OFFSETS[1:])
    ]
    matrix, both = pair_matrix(place, pairs, weights, count, groups)
    params = pltpu.CompilerParams(vmem_limit_bytes=VMEM)
    result = jax.ShapeDtypeStruct(conductivity.shape, jnp.float32)

    def lowest(some):
        plane = jnp.stack([block[0, :planes] for block in some])
        return lax.ppermute(plane, "slab", [(i + 1, i) for i in range(slabs - 1)])

    some = lax.optimization_barrier((*blocks[:EARLY], matrix))
    above = lowest(some[:-1])
    early = pl.pallas_call(
        early_kernel,
        out_shape=result,
        compiler_params=params,
        cost_estimate=pl.CostEstimate(flops=900000000, bytes_accessed=3000000, transcendentals=0),
        name="early_slopes",
    )(matrix, *blocks[:EARLY])
    rest, early = lax.optimization_barrier((tuple(blocks[EARLY:]), early))
    late_above = lowest(rest)
    inner, mixed = pl.pallas_call(
        functools.partial(late_kernel, EARLY),
        out_shape=[
            result,
            jax.ShapeDtypeStruct(
                (planes, sum(block.shape[2] for block in rest), conductivity.shape[2]), jnp.float32
            ),
        ],
        compiler_params=params,
        cost_estimate=pl.CostEstimate(flops=700000000, bytes_accessed=3000000, transcendentals=0),
        name="late_slopes",
    )(matrix, both, early, above, *blocks)
    return pl.pallas_call(
        functools.partial(outer_kernel, EARLY),
        out_shape=result,
        compiler_params=params,
        name="outer_slopes",
    )(matrix, inner, mixed, conductivity, late_above, *blocks[EARLY:])


def solution(mesh):
    return jax.shard_map(
        body,
        mesh=mesh,
        in_specs=(
            P("elec", None, "slab", None),
            P("elec", "slab", None),
            P(None, "elec"),
            P(),
            P(),
        ),
        out_specs=P("elec", "slab", None),
        check_vma=False,
    )
```

```python
import functools

import jax
import jax.numpy as jnp
from jax import lax
from jax.experimental import pallas as pl
from jax.experimental.pallas import tpu as pltpu
from jax.sharding import PartitionSpec as P

VMEM = 40 * 1024 * 1024
PAIR_STEP = 8192
HALO_ROWS = 16
EARLY = 6
OFFSETS = [(0, 0), (2, 0), (0, 1), (2, 1), (1, 1), (3, 0), (3, 1), (1, 0)]


def partner(me, offset, groups):
    y_step, flip = offset
    return (me // 2 + y_step) % (groups // 2) * 2 + (me % 2 + flip) % 2


def origin(me, offset, groups):
    return partner(me, ((groups // 2 - offset[0]) % (groups // 2), offset[1]), groups)


def column(row):
    count = row.shape[1]
    own = lax.broadcasted_iota(jnp.int32, (count, count), 0) == lax.broadcasted_iota(jnp.int32, (count, count), 1)
    return jnp.sum(jnp.where(own, jnp.broadcast_to(row, (count, count)), 0.0), axis=1, keepdims=True)


def fields_kernel(offsets, groups, nz, place_ref, positions_ref, rows_ref, *refs):
    outs = refs
    me, z_first = place_ref[0], place_ref[1] * nz
    count, width = rows_ref.shape[0], rows_ref.shape[2]
    total = rows_ref.shape[1]
    planes = total // nz // groups
    targets = [partner(me, offset, groups) for offset in offsets]

    places = positions_ref[...].astype(jnp.float32)
    x_place, z_place, y_place = (column(places[axis : axis + 1]) for axis in range(3))
    y_gap = lax.broadcasted_iota(jnp.int32, (count, width), 1).astype(jnp.float32) - y_place
    y_part = y_gap * y_gap + 0.5
    z_parts = []
    for z in range(nz):
        z_gap = (z_first + z).astype(jnp.float32) - z_place
        z_parts.append(z_gap * z_gap + y_part)

    def planes_of(pair, x_first, keep):
        turned = jnp.swapaxes(pair.astype(jnp.float32), 0, 1)
        for step in range(keep):
            x_gap = (x_first + step).astype(jnp.float32) - x_place
            x_part = x_gap * x_gap
            for z in range(nz):
                value = turned[step * nz + z] + 4.0 * lax.rsqrt(z_parts[z] + x_part)
                yield step, z, value.astype(jnp.bfloat16)

    for slot, target in enumerate(targets):
        out_ref = outs[slot]
        start = pl.multiple_of(target * (planes * nz), planes * nz)
        after = pl.multiple_of(jnp.minimum(start + planes * nz, total - HALO_ROWS), HALO_ROWS)
        for first in range(0, planes, 2):
            pair = rows_ref[:, pl.ds(start + first * nz, 2 * nz), :]
            for step, z, value in planes_of(pair, target * planes + first, 2):
                out_ref[z, first + step] = value
        last = target == groups - 1
        for _, z, value in planes_of(rows_ref[:, pl.ds(after, 2 * nz), :], (target + 1) * planes, 1):
            out_ref[z, planes] = jnp.where(last, jnp.zeros_like(value), value)


def spread_fields(offsets, place, secondary, positions, groups):
    count, nx, nz, ny = secondary.shape
    planes = nx // groups
    slots = len(offsets)
    rows = secondary.reshape(count, nx * nz, ny)
    return pl.pallas_call(
        functools.partial(fields_kernel, offsets, groups, nz),
        in_specs=[
            pl.BlockSpec(memory_space=pltpu.SMEM),
            pl.BlockSpec(memory_space=pltpu.VMEM),
            pl.BlockSpec(memory_space=pltpu.VMEM),
        ],
        out_specs=[pl.BlockSpec(memory_space=pltpu.VMEM)] * slots,
        out_shape=[jax.ShapeDtypeStruct((nz, planes + 1, count, ny), jnp.bfloat16)] * slots,
        compiler_params=pltpu.CompilerParams(vmem_limit_bytes=VMEM),
        name="fields",
    )(place, positions, rows)


def pairs_kernel(groups, count, place_ref, pairs_ref, weights_ref, out_ref, both_ref, total_ref):
    total_ref[...] = jnp.zeros_like(total_ref)
    part = count // groups
    ids = []
    for offset in OFFSETS:
        first = origin(place_ref[0], offset, groups) * part
        ids.append(lax.broadcasted_iota(jnp.int32, (part, PAIR_STEP), 0) + first)
    ids = jnp.concatenate(ids, axis=0)

    @pl.loop(0, pairs_ref.shape[1] // PAIR_STEP)
    def _(step):
        span = pl.ds(pl.multiple_of(step * PAIR_STEP, PAIR_STEP), PAIR_STEP)
        weight = weights_ref[:, span]
        high = weight.astype(jnp.bfloat16).astype(jnp.float32)
        source = ids == pairs_ref[0:1, span]
        target = jnp.where(ids == pairs_ref[1:2, span], 1.0, 0.0).astype(jnp.bfloat16)
        for term in (high, weight - high):
            hot = jnp.where(source, term, 0.0).astype(jnp.bfloat16)
            total_ref[...] += lax.dot_general(
                hot, target, (((1,), (1,)), ((), ())), preferred_element_type=jnp.float32
            )

    out_ref[...] = total_ref[...].astype(jnp.bfloat16)
    both_ref[...] = (total_ref[...] + jnp.transpose(total_ref[...])).astype(jnp.bfloat16)


def pair_matrix(place, pairs, weights, count, groups):
    return pl.pallas_call(
        functools.partial(pairs_kernel, groups, count),
        in_specs=[
            pl.BlockSpec(memory_space=pltpu.SMEM),
            pl.BlockSpec(memory_space=pltpu.VMEM),
            pl.BlockSpec(memory_space=pltpu.VMEM),
        ],
        out_shape=[jax.ShapeDtypeStruct((count, count), jnp.bfloat16)] * 2,
        scratch_shapes=[pltpu.VMEM((count, count), jnp.float32)],
        compiler_params=pltpu.CompilerParams(vmem_limit_bytes=VMEM),
        cost_estimate=pl.CostEstimate(
            flops=4 * pairs.shape[0] * count * count, bytes_accessed=12 * pairs.shape[0], transcendentals=0
        ),
        name="pair_weights",
    )(place, pairs.T, weights.reshape(1, -1))


def forms(matrix, slopes, first=0):
    flat = [(key, slope) for key, some in slopes.items() for slope in some]
    totals = {}
    for at in range(0, len(flat), 2):
        pair = flat[at : at + 2]
        width = pair[0][1].shape[1]
        mixed = jnp.dot(
            matrix, jnp.concatenate([slope for _, slope in pair], axis=1), preferred_element_type=jnp.float32
        )
        for index, (key, slope) in enumerate(pair):
            term = slope[first:].astype(jnp.float32) * mixed[:, index * width : (index + 1) * width]
            totals[key] = totals[key] + term if key in totals else term
    return {key: jnp.sum(total, axis=0) for key, total in totals.items()}


def node_slopes(blocks, x, z):
    nz = blocks[0].shape[0]

    def field(x, z):
        return jnp.concatenate([block[z, x] for block in blocks], axis=0)

    here = field(x, z)
    ahead = jnp.concatenate([here[:, 1:], jnp.zeros((here.shape[0], 1), here.dtype)], axis=1)
    slopes = [field(x + 1, z) - here, ahead - here]
    if z < nz - 1:
        slopes.append(field(x, z + 1) - here)
    return slopes


def early_kernel(matrix_ref, *refs):
    blocks, out_ref = refs[:-1], refs[-1]
    nz, planes, part, _ = blocks[0].shape
    count = part * len(blocks)
    matrix = matrix_ref[:count, :count]

    @pl.loop(0, (planes - 1) // 2)
    def _(half):
        nodes = [(2 * half + step, step, z) for step in range(2) for z in range(nz)]
        sums = forms(matrix, {(step, z): node_slopes(blocks, x, z) for x, step, z in nodes})
        for x, step, z in nodes:
            out_ref[x, z] = sums[step, z]


def late_kernel(early, matrix_ref, both_ref, early_ref, above_ref, *refs):
    blocks, (out_ref, mixed_ref) = refs[:-2], refs[-2:]
    nz, planes, part, _ = blocks[0].shape
    first = early * part
    matrix = jnp.concatenate([both_ref[first:, :first], matrix_ref[first:, first:]], axis=1)
    rows = jnp.concatenate([matrix_ref[:first, :first], both_ref[first:, :first]], axis=0)

    def rise(x):
        return jnp.concatenate([above_ref[slot, x] - blocks[slot][nz - 1, x] for slot in range(early)], axis=0)

    @pl.loop(0, (planes - 1) // 2)
    def _(half):
        nodes = [(2 * half + step, step, z) for step in range(2) for z in range(nz)]
        sums = forms(matrix, {(step, z): node_slopes(blocks, x, z) for x, step, z in nodes}, first)
        rises = [rise(2 * half + step) for step in range(2)]
        width = rises[0].shape[1]
        mixed = jnp.dot(rows, jnp.concatenate(rises, axis=1), preferred_element_type=jnp.float32)
        for x, step, z in nodes:
            value = early_ref[x, z] + sums[step, z]
            if z == nz - 1:
                own = mixed[:, step * width : (step + 1) * width]
                value += jnp.sum(rises[step].astype(jnp.float32) * own[:first], axis=0)
                mixed_ref[x] = own[first:]
            out_ref[x, z] = value


def outer_kernel(early, matrix_ref, inner_ref, mixed_ref, conductivity_ref, above_ref, *refs):
    blocks, out_ref = refs[:-1], refs[-1]
    planes = above_ref.shape[1]
    top, part = blocks[0].shape[0] - 1, blocks[0].shape[2]
    first = early * part
    matrix = matrix_ref[first:, first:]
    for x in range(0, planes, 2):
        slopes = [
            jnp.concatenate([above_ref[slot, x + step] - block[top, x + step] for slot, block in enumerate(blocks)], axis=0)
            for step in range(2)
        ]
        width = slopes[0].shape[1]
        mixed = jnp.dot(matrix, jnp.concatenate(slopes, axis=1), preferred_element_type=jnp.float32)
        for step in range(2):
            own = mixed_ref[x + step] + mixed[:, step * width : (step + 1) * width]
            rise = jnp.sum(slopes[step].astype(jnp.float32) * own, axis=0)
            for z in range(top):
                out_ref[x + step, z] = conductivity_ref[x + step, z] * inner_ref[x + step, z]
            out_ref[x + step, top] = conductivity_ref[x + step, top] * (inner_ref[x + step, top] + rise)


def body(secondary, conductivity, positions, pairs, weights):
    groups = lax.axis_size("elec")
    slabs = lax.axis_size("slab")
    count = secondary.shape[0] * groups
    place = jnp.stack([lax.axis_index("elec"), lax.axis_index("slab")])
    nodes = positions.astype(jnp.float32)
    blocks = list(spread_fields(OFFSETS[1:], place, secondary, nodes, groups))
    blocks = list(spread_fields(OFFSETS[:1], place, secondary, nodes, groups)) + blocks
    planes = blocks[0].shape[1] - 1
    blocks = [blocks[0]] + [
        lax.ppermute(block, "elec", [(i, partner(i, offset, groups)) for i in range(groups)])
        for block, offset in zip(blocks[1:], OFFSETS[1:])
    ]
    matrix, both = pair_matrix(place, pairs, weights, count, groups)
    params = pltpu.CompilerParams(vmem_limit_bytes=VMEM)
    result = jax.ShapeDtypeStruct(conductivity.shape, jnp.float32)

    def lowest(some):
        plane = jnp.stack([block[0, :planes] for block in some])
        return lax.ppermute(plane, "slab", [(i + 1, i) for i in range(slabs - 1)])

    some = lax.optimization_barrier((*blocks[:EARLY], matrix))
    above = lowest(some[:-1])
    early = pl.pallas_call(
        early_kernel,
        out_shape=result,
        compiler_params=params,
        cost_estimate=pl.CostEstimate(flops=900000000, bytes_accessed=3000000, transcendentals=0),
        name="early_slopes",
    )(matrix, *blocks[:EARLY])
    rest, early = lax.optimization_barrier((tuple(blocks[EARLY:]), early))
    late_above = lowest(rest)
    inner, mixed = pl.pallas_call(
        functools.partial(late_kernel, EARLY),
        out_shape=[
            result,
            jax.ShapeDtypeStruct(
                (planes, sum(block.shape[2] for block in rest), conductivity.shape[2]), jnp.float32
            ),
        ],
        compiler_params=params,
        cost_estimate=pl.CostEstimate(flops=700000000, bytes_accessed=3000000, transcendentals=0),
        name="late_slopes",
    )(matrix, both, early, above, *blocks)
    return pl.pallas_call(
        functools.partial(outer_kernel, EARLY),
        out_shape=result,
        compiler_params=params,
        name="outer_slopes",
    )(matrix, inner, mixed, conductivity, late_above, *blocks[EARLY:])


def solution(mesh):
    return jax.shard_map(
        body,
        mesh=mesh,
        in_specs=(
            P("elec", None, "slab", None),
            P("elec", "slab", None),
            P(None, "elec"),
            P(),
            P(),
        ),
        out_specs=P("elec", "slab", None),
        check_vma=False,
    )
```

```python
import functools

import jax
import jax.numpy as jnp
from jax import lax
from jax.experimental import pallas as pl
from jax.experimental.pallas import tpu as pltpu
from jax.sharding import PartitionSpec as P

VMEM = 40 * 1024 * 1024
PAIR_STEP = 8192
HALO_ROWS = 16
EARLY = 6
OFFSETS = [(0, 0), (1, 1), (3, 0), (0, 1), (2, 0), (2, 1), (3, 1), (1, 0)]


def partner(me, offset, groups):
    y_step, flip = offset
    return (me // 2 + y_step) % (groups // 2) * 2 + (me % 2 + flip) % 2


def origin(me, offset, groups):
    return partner(me, ((groups // 2 - offset[0]) % (groups // 2), offset[1]), groups)


def column(row):
    count = row.shape[1]
    own = lax.broadcasted_iota(jnp.int32, (count, count), 0) == lax.broadcasted_iota(jnp.int32, (count, count), 1)
    return jnp.sum(jnp.where(own, jnp.broadcast_to(row, (count, count)), 0.0), axis=1, keepdims=True)


def fields_kernel(offsets, groups, nz, place_ref, positions_ref, rows_ref, *refs):
    outs = refs
    me, z_first = place_ref[0], place_ref[1] * nz
    count, width = rows_ref.shape[0], rows_ref.shape[2]
    total = rows_ref.shape[1]
    planes = total // nz // groups
    targets = [partner(me, offset, groups) for offset in offsets]

    places = positions_ref[...].astype(jnp.float32)
    x_place, z_place, y_place = (column(places[axis : axis + 1]) for axis in range(3))
    y_gap = lax.broadcasted_iota(jnp.int32, (count, width), 1).astype(jnp.float32) - y_place
    y_part = y_gap * y_gap + 0.5
    z_parts = []
    for z in range(nz):
        z_gap = (z_first + z).astype(jnp.float32) - z_place
        z_parts.append(z_gap * z_gap + y_part)

    def planes_of(pair, x_first, keep):
        turned = jnp.swapaxes(pair.astype(jnp.float32), 0, 1)
        for step in range(keep):
            x_gap = (x_first + step).astype(jnp.float32) - x_place
            x_part = x_gap * x_gap
            for z in range(nz):
                value = turned[step * nz + z] + 4.0 * lax.rsqrt(z_parts[z] + x_part)
                yield step, z, value.astype(jnp.bfloat16)

    for slot, target in enumerate(targets):
        out_ref = outs[slot]
        start = pl.multiple_of(target * (planes * nz), planes * nz)
        after = pl.multiple_of(jnp.minimum(start + planes * nz, total - HALO_ROWS), HALO_ROWS)
        for first in range(0, planes, 2):
            pair = rows_ref[:, pl.ds(start + first * nz, 2 * nz), :]
            for step, z, value in planes_of(pair, target * planes + first, 2):
                out_ref[z, first + step] = value
        last = target == groups - 1
        for _, z, value in planes_of(rows_ref[:, pl.ds(after, 2 * nz), :], (target + 1) * planes, 1):
            out_ref[z, planes] = jnp.where(last, jnp.zeros_like(value), value)


def spread_fields(offsets, place, secondary, positions, groups):
    count, nx, nz, ny = secondary.shape
    planes = nx // groups
    slots = len(offsets)
    rows = secondary.reshape(count, nx * nz, ny)
    return pl.pallas_call(
        functools.partial(fields_kernel, offsets, groups, nz),
        in_specs=[
            pl.BlockSpec(memory_space=pltpu.SMEM),
            pl.BlockSpec(memory_space=pltpu.VMEM),
            pl.BlockSpec(memory_space=pltpu.VMEM),
        ],
        out_specs=[pl.BlockSpec(memory_space=pltpu.VMEM)] * slots,
        out_shape=[jax.ShapeDtypeStruct((nz, planes + 1, count, ny), jnp.bfloat16)] * slots,
        compiler_params=pltpu.CompilerParams(vmem_limit_bytes=VMEM),
        name="fields",
    )(place, positions, rows)


def pairs_kernel(groups, count, place_ref, pairs_ref, weights_ref, out_ref, both_ref, total_ref):
    total_ref[...] = jnp.zeros_like(total_ref)
    part = count // groups
    ids = []
    for offset in OFFSETS:
        first = origin(place_ref[0], offset, groups) * part
        ids.append(lax.broadcasted_iota(jnp.int32, (part, PAIR_STEP), 0) + first)
    ids = jnp.concatenate(ids, axis=0)

    @pl.loop(0, pairs_ref.shape[1] // PAIR_STEP)
    def _(step):
        span = pl.ds(pl.multiple_of(step * PAIR_STEP, PAIR_STEP), PAIR_STEP)
        weight = weights_ref[:, span]
        high = weight.astype(jnp.bfloat16).astype(jnp.float32)
        source = ids == pairs_ref[0:1, span]
        target = jnp.where(ids == pairs_ref[1:2, span], 1.0, 0.0).astype(jnp.bfloat16)
        for term in (high, weight - high):
            hot = jnp.where(source, term, 0.0).astype(jnp.bfloat16)
            total_ref[...] += lax.dot_general(
                hot, target, (((1,), (1,)), ((), ())), preferred_element_type=jnp.float32
            )

    out_ref[...] = total_ref[...].astype(jnp.bfloat16)
    both_ref[...] = (total_ref[...] + jnp.transpose(total_ref[...])).astype(jnp.bfloat16)


def pair_matrix(place, pairs, weights, count, groups):
    return pl.pallas_call(
        functools.partial(pairs_kernel, groups, count),
        in_specs=[
            pl.BlockSpec(memory_space=pltpu.SMEM),
            pl.BlockSpec(memory_space=pltpu.VMEM),
            pl.BlockSpec(memory_space=pltpu.VMEM),
        ],
        out_shape=[jax.ShapeDtypeStruct((count, count), jnp.bfloat16)] * 2,
        scratch_shapes=[pltpu.VMEM((count, count), jnp.float32)],
        compiler_params=pltpu.CompilerParams(vmem_limit_bytes=VMEM),
        cost_estimate=pl.CostEstimate(
            flops=4 * pairs.shape[0] * count * count, bytes_accessed=12 * pairs.shape[0], transcendentals=0
        ),
        name="pair_weights",
    )(place, pairs.T, weights.reshape(1, -1))


def forms(matrix, slopes, first=0):
    flat = [(key, slope) for key, some in slopes.items() for slope in some]
    totals = {}
    for at in range(0, len(flat), 2):
        pair = flat[at : at + 2]
        width = pair[0][1].shape[1]
        mixed = jnp.dot(
            matrix, jnp.concatenate([slope for _, slope in pair], axis=1), preferred_element_type=jnp.float32
        )
        for index, (key, slope) in enumerate(pair):
            term = slope[first:].astype(jnp.float32) * mixed[:, index * width : (index + 1) * width]
            totals[key] = totals[key] + term if key in totals else term
    return {key: jnp.sum(total, axis=0) for key, total in totals.items()}


def node_slopes(blocks, x, z):
    nz = blocks[0].shape[0]

    def field(x, z):
        return jnp.concatenate([block[z, x] for block in blocks], axis=0)

    here = field(x, z)
    ahead = jnp.concatenate([here[:, 1:], jnp.zeros((here.shape[0], 1), here.dtype)], axis=1)
    slopes = [field(x + 1, z) - here, ahead - here]
    if z < nz - 1:
        slopes.append(field(x, z + 1) - here)
    return slopes


def early_kernel(matrix_ref, *refs):
    blocks, out_ref = refs[:-1], refs[-1]
    nz, planes, part, _ = blocks[0].shape
    count = part * len(blocks)
    matrix = matrix_ref[:count, :count]

    @pl.loop(0, (planes - 1) // 2)
    def _(half):
        nodes = [(2 * half + step, step, z) for step in range(2) for z in range(nz)]
        sums = forms(matrix, {(step, z): node_slopes(blocks, x, z) for x, step, z in nodes})
        for x, step, z in nodes:
            out_ref[x, z] = sums[step, z]


def late_kernel(early, matrix_ref, both_ref, early_ref, above_ref, *refs):
    blocks, (out_ref, mixed_ref) = refs[:-2], refs[-2:]
    nz, planes, part, _ = blocks[0].shape
    first = early * part
    matrix = jnp.concatenate([both_ref[first:, :first], matrix_ref[first:, first:]], axis=1)
    rows = jnp.concatenate([matrix_ref[:first, :first], both_ref[first:, :first]], axis=0)

    def rise(x):
        return jnp.concatenate([above_ref[slot, x] - blocks[slot][nz - 1, x] for slot in range(early)], axis=0)

    @pl.loop(0, (planes - 1) // 2)
    def _(half):
        nodes = [(2 * half + step, step, z) for step in range(2) for z in range(nz)]
        sums = forms(matrix, {(step, z): node_slopes(blocks, x, z) for x, step, z in nodes}, first)
        rises = [rise(2 * half + step) for step in range(2)]
        width = rises[0].shape[1]
        mixed = jnp.dot(rows, jnp.concatenate(rises, axis=1), preferred_element_type=jnp.float32)
        for x, step, z in nodes:
            value = early_ref[x, z] + sums[step, z]
            if z == nz - 1:
                own = mixed[:, step * width : (step + 1) * width]
                value += jnp.sum(rises[step].astype(jnp.float32) * own[:first], axis=0)
                mixed_ref[x] = own[first:]
            out_ref[x, z] = value


def outer_kernel(early, matrix_ref, inner_ref, mixed_ref, conductivity_ref, above_ref, *refs):
    blocks, out_ref = refs[:-1], refs[-1]
    planes = above_ref.shape[1]
    top, part = blocks[0].shape[0] - 1, blocks[0].shape[2]
    first = early * part
    matrix = matrix_ref[first:, first:]
    for x in range(0, planes, 2):
        slopes = [
            jnp.concatenate([above_ref[slot, x + step] - block[top, x + step] for slot, block in enumerate(blocks)], axis=0)
            for step in range(2)
        ]
        width = slopes[0].shape[1]
        mixed = jnp.dot(matrix, jnp.concatenate(slopes, axis=1), preferred_element_type=jnp.float32)
        for step in range(2):
            own = mixed_ref[x + step] + mixed[:, step * width : (step + 1) * width]
            rise = jnp.sum(slopes[step].astype(jnp.float32) * own, axis=0)
            for z in range(top):
                out_ref[x + step, z] = conductivity_ref[x + step, z] * inner_ref[x + step, z]
            out_ref[x + step, top] = conductivity_ref[x + step, top] * (inner_ref[x + step, top] + rise)


def body(secondary, conductivity, positions, pairs, weights):
    groups = lax.axis_size("elec")
    slabs = lax.axis_size("slab")
    count = secondary.shape[0] * groups
    place = jnp.stack([lax.axis_index("elec"), lax.axis_index("slab")])
    nodes = positions.astype(jnp.float32)
    blocks = list(spread_fields(OFFSETS[1:], place, secondary, nodes, groups))
    blocks = list(spread_fields(OFFSETS[:1], place, secondary, nodes, groups)) + blocks
    planes = blocks[0].shape[1] - 1
    blocks = [blocks[0]] + [
        lax.ppermute(block, "elec", [(i, partner(i, offset, groups)) for i in range(groups)])
        for block, offset in zip(blocks[1:], OFFSETS[1:])
    ]
    matrix, both = pair_matrix(place, pairs, weights, count, groups)
    params = pltpu.CompilerParams(vmem_limit_bytes=VMEM)
    result = jax.ShapeDtypeStruct(conductivity.shape, jnp.float32)

    def lowest(some):
        plane = jnp.stack([block[0, :planes] for block in some])
        return lax.ppermute(plane, "slab", [(i + 1, i) for i in range(slabs - 1)])

    some = lax.optimization_barrier((*blocks[:EARLY], matrix))
    above = lowest(some[:-1])
    early = pl.pallas_call(
        early_kernel,
        out_shape=result,
        compiler_params=params,
        cost_estimate=pl.CostEstimate(flops=900000000, bytes_accessed=3000000, transcendentals=0),
        name="early_slopes",
    )(matrix, *blocks[:EARLY])
    rest, early = lax.optimization_barrier((tuple(blocks[EARLY:]), early))
    late_above = lowest(rest)
    inner, mixed = pl.pallas_call(
        functools.partial(late_kernel, EARLY),
        out_shape=[
            result,
            jax.ShapeDtypeStruct(
                (planes, sum(block.shape[2] for block in rest), conductivity.shape[2]), jnp.float32
            ),
        ],
        compiler_params=params,
        cost_estimate=pl.CostEstimate(flops=700000000, bytes_accessed=3000000, transcendentals=0),
        name="late_slopes",
    )(matrix, both, early, above, *blocks)
    return pl.pallas_call(
        functools.partial(outer_kernel, EARLY),
        out_shape=result,
        compiler_params=params,
        name="outer_slopes",
    )(matrix, inner, mixed, conductivity, late_above, *blocks[EARLY:])


def solution(mesh):
    return jax.shard_map(
        body,
        mesh=mesh,
        in_specs=(
            P("elec", None, "slab", None),
            P("elec", "slab", None),
            P(None, "elec"),
            P(),
            P(),
        ),
        out_specs=P("elec", "slab", None),
        check_vma=False,
    )
```
